256 devices in a mesh: batch: 2 (over x_hi), ctx: 128 (over y, z, x_lo, core).
Axes of the slice: x: 4 (x_hi: 2, x_lo: 2; x = x_hi * 2 + x_lo), y: 4, z: 8, core: 2. Of those that a mesh axis runs over, the one named last changes fastest.
Arguments:
- queries: bfloat16 [1024, 4096], P(('batch', 'ctx')), parts along dimension 0, may hold values from -24 to 24
- owners: int32 [512, 1], P('batch'), parts along dimension 0, may hold values from 0 to 127; in each aligned block of 256 rows (0 to 255, 256 to 511, ...) at most 4 rows name the same one
- new_keys: bfloat16 [1024, 1024], P(('batch', 'ctx')), parts along dimension 0, may hold values from -6 to 6
- new_values: bfloat16 [1024, 1024], P(('batch', 'ctx')), parts along dimension 0, may hold values from -6 to 6
- cache_keys: bfloat16 [65536, 1024], P(('batch', 'ctx')), parts along dimension 0, may hold values from -16 to 16
- cache_values: bfloat16 [65536, 1024], P(('batch', 'ctx')), parts along dimension 0, may hold values from -6 to 6
- lengths: int32 [256], P(('batch', 'ctx')), parts along dimension 0, may hold values from 1 to 256, as said below
Outputs:
- attended: bfloat16 [1024, 4096], P(('batch', 'ctx')), parts along dimension 0
The draws below stay inside these ranges and needn't reach their ends.
There are 2 independent parts, one for each index of `batch`. The reference program is written for one: setup_inputs(seed, part) draws one part's arguments, and reference() takes and returns one part's arrays. A program takes and returns all parts, laid end to end along the dimension named above; each array names one. Nothing has to cross between parts.
Inputs may be any that keep to these rules, and one draw needn't show every extreme that they name: `owners`: at most 4 new tokens on one device, exactly 4 on some device. `lengths`: the live slots of a device are its first ones; some device is full.
All inputs are finite; a program needn't handle non-finite values.
Results may differ from the reference program's by a relative error of at most 0.003.
Values may be sent and summed in bfloat16 or wider, within the bound.
No kernel may reach another device: no remote copies, remote signals or barrier semaphores. Data moves between devices by JAX's collectives and lax.ppermute only.
A program may use at most 128 MiB of HBM per device.

```python
import math
import jax
import jax.numpy as jnp
import numpy as np
from jax import lax

QUERY_HEADS = 32
KEY_VALUE_HEADS = 8
HEAD_DIMENSION = 128
CTX_DEV = 256
TOKEN_SLOTS = 4
NEW = 256
CACHE = 32768
KW = 1024
N_CTX = 128


def draw_queries(key, part):
    key = jax.random.fold_in(key, 11)
    query_rows = N_CTX * TOKEN_SLOTS
    value_rows = 3.0 * jnp.clip(jax.random.normal(key, (query_rows, QUERY_HEADS * HEAD_DIMENSION), jnp.float32), -4.0, 4.0)
    return value_rows.astype(jnp.bfloat16)


def draw_cache_keys(key, part):
    key = jax.random.fold_in(key, 12)
    whole_length = N_CTX * CTX_DEV
    value_rows = jnp.clip(jax.random.normal(key, (whole_length, KEY_VALUE_HEADS * HEAD_DIMENSION), jnp.float32), -4.0, 4.0)
    return value_rows.astype(jnp.bfloat16)


def draw_lengths(key, part):
    key = jax.random.fold_in(key, 13)
    halvings = jax.random.randint(jax.random.fold_in(key, 1), (N_CTX,), 0, 4)
    base_offset = (CTX_DEV // jnp.power(2, halvings)).astype(jnp.int32)
    trim = jax.random.randint(jax.random.fold_in(key, 2), (N_CTX,), 0, base_offset // 4 + 1)
    result = (base_offset - trim).astype(jnp.int32)
    fullest = jax.random.randint(jax.random.fold_in(key, 3), (), 0, N_CTX)
    result = result.at[fullest].set(CTX_DEV)
    return result.astype(jnp.int32)


def level_of(key, extent, split, least, top_value):
    gain = 1.0
    for dim, shards_of in split:
        draws = jax.random.uniform(jax.random.fold_in(jax.random.fold_in(key, 6), dim), (shards_of,), jnp.float32, least / len(split), top_value / len(split))
        gain = gain * jnp.repeat(jnp.exp(draws), extent[dim] // shards_of).reshape((-1,) + (1,) * (len(extent) - 1 - dim))
    return gain


def routed_block(own_key, own, number, rows, number_of, top, most, lean):
    order = jax.random.permutation(own_key, number_of)
    heavy_load, ordinary = shares(number_of, rows * top, most, lean, True), shares(number_of, rows * top, most, lean, False)
    places = jnp.arange(number_of)

    def named(sizes, offset_by):
        used = int((sizes > 0).sum())
        fixed = max(1, used // 4)
        moved = fixed + (places - fixed + offset_by * (used - fixed)) % max(1, number_of - fixed)
        return jnp.zeros((number_of,), jnp.int32).at[order[jnp.where(places < fixed, places, moved)]].set(jnp.asarray(sizes, jnp.int32))

    sizes = jnp.where(number % 4 == 0, named(heavy_load, number // 4), named(ordinary, number - number // 4 - 1))
    mixed = jax.random.permutation(jax.random.fold_in(own, 3), number_of)
    giver, taker = mixed[0:number_of // 2 * 2:2], mixed[1:number_of // 2 * 2:2]
    slack = jnp.minimum(sizes[giver] - 1, most - sizes[taker]) // 2
    slack = jnp.where((giver == order[0]) | (taker == order[0]) | (sizes[taker] == 0), 0, jnp.maximum(slack, 0))
    moved = jax.random.randint(jax.random.fold_in(own, 4), (number_of // 2,), 0, 1 << 20) % (slack + 1)
    sizes = sizes.at[giver].add(-moved).at[taker].add(moved)
    items = jnp.searchsorted(jnp.cumsum(sizes), jnp.arange(rows * top), side="right").astype(jnp.int32)
    table = items.reshape(top, rows).T
    table = table[jax.random.permutation(jax.random.fold_in(own, 1), rows)]
    offset_by = jax.random.randint(jax.random.fold_in(own, 2), (rows, 1), 0, top)
    return jnp.take_along_axis(table, (jnp.arange(top)[None, :] + offset_by) % top, axis=1)


def shares(amount, total, bound, slope, full):
    portions = [(1 << 20) // math.isqrt(grade ** slope) + 1 for grade in range(1, amount + 1)]
    largest = bound if full else min(bound, max(-(-total // amount), total * portions[0] // sum(portions)))
    least = 1 if total - largest >= amount - 1 else 0
    given, spare = [largest] + [least] * (amount - 1), total - largest - least * (amount - 1)
    while spare > 0:
        movable = [i for i in range(1, amount) if given[i] < largest] or [i for i in range(1, amount) if given[i] < bound]
        mass, budget = sum([portions[i] for i in movable]), spare
        for i in movable:
            more = min(bound - given[i], max(1, budget * portions[i] // mass), spare)
            given[i] = given[i] + more
            spare = spare - more
    return np.array(given)


def normal_values(own_key, shape, width, reach, split=(), held_as=jnp.bfloat16):
    values = width * jax.random.normal(own_key, shape, jnp.float32)
    if split:
        values = values * level_of(own_key, shape, split, -0.22, 0.18)
    return jnp.clip(values, -reach, reach).astype(held_as)


def setup_inputs(seed: int = 0, part: int = 0) -> dict:
    key_list = jax.random.split(jax.random.key(seed), 8)
    own_keys = jax.random.split(jax.random.fold_in(key_list[7], part), 8)
    queries = draw_queries(jax.random.fold_in(jax.random.fold_in(key_list[7], part), 71), part)
    owners_keys = jax.random.split(jax.random.fold_in(own_keys[1], 1), NEW // NEW)
    owners_turns = jax.random.permutation(jax.random.fold_in(own_keys[1], 3), NEW // NEW)
    owners = jax.vmap(lambda own, number: routed_block(jax.random.fold_in(own_keys[1], 2), own, number, NEW, N_CTX, 1, TOKEN_SLOTS, 2))(owners_keys, owners_turns).reshape((NEW, 1))
    new_keys = normal_values(own_keys[2], (N_CTX * TOKEN_SLOTS, KW), 1.5, 6.0, ((0, 128),))
    new_values = normal_values(own_keys[3], (N_CTX * TOKEN_SLOTS, KW), 1.0, 6.0, ((0, 128),))
    cache_keys = draw_cache_keys(jax.random.fold_in(jax.random.fold_in(key_list[7], part), 71), part)
    cache_values = normal_values(own_keys[5], (CACHE, KW), 1.0, 6.0, ((0, 128),))
    lengths = draw_lengths(jax.random.fold_in(jax.random.fold_in(key_list[7], part), 71), part)
    return dict(queries=queries, owners=owners, new_keys=new_keys, new_values=new_values, cache_keys=cache_keys, cache_values=cache_values, lengths=lengths)


def slot_tokens(owners, count, slots):
    owner_col = owners[:, 0].astype(jnp.int32)
    devices = jnp.arange(count, dtype=jnp.int32)
    onehot = (owner_col[:, None] == devices[None, :]).astype(jnp.int32)
    earlier = (jnp.cumsum(onehot, axis=0) - onehot).astype(jnp.int32)
    rank = lax.optimization_barrier(jnp.sum(earlier * onehot, axis=1)).astype(jnp.int32)
    placed = (owner_col * slots + rank).astype(jnp.int32)
    tokens = jnp.arange(owner_col.shape[0], dtype=jnp.int32)
    return jnp.full((count * slots,), -1, jnp.int32).at[placed].set(tokens)

def block_terms(queries, query_tokens, keys, value_rows, live, new_keys, new_values, new_tokens):
    query_rows = queries.shape[0]
    head_group = QUERY_HEADS // KEY_VALUE_HEADS
    scale = 1.0 / math.sqrt(HEAD_DIMENSION)
    cache_mask = (jnp.arange(keys.shape[0], dtype=jnp.int32) < live)[None, None, :]
    new_mask = ((new_tokens[None, :] >= 0) & (new_tokens[None, :] <= query_tokens[:, None]))[:, None, :]
    outputs, peaks, totals = ([], [], [])
    for head_index in range(KEY_VALUE_HEADS):
        query = queries[:, head_index * head_group * HEAD_DIMENSION:(head_index + 1) * head_group * HEAD_DIMENSION].reshape(query_rows, head_group, HEAD_DIMENSION).astype(jnp.float32)
        key_old = keys[:, head_index * HEAD_DIMENSION:(head_index + 1) * HEAD_DIMENSION].astype(jnp.float32)
        value_old = value_rows[:, head_index * HEAD_DIMENSION:(head_index + 1) * HEAD_DIMENSION].astype(jnp.float32)
        key_new = new_keys[:, head_index * HEAD_DIMENSION:(head_index + 1) * HEAD_DIMENSION].astype(jnp.float32)
        value_new = new_values[:, head_index * HEAD_DIMENSION:(head_index + 1) * HEAD_DIMENSION].astype(jnp.float32)
        score_old = jnp.einsum('rhd,kd->rhk', query, key_old, preferred_element_type=jnp.float32) * scale
        score_new = jnp.einsum('rhd,kd->rhk', query, key_new, preferred_element_type=jnp.float32) * scale
        score_old = jnp.where(cache_mask, score_old, -1e+30)
        score_new = jnp.where(new_mask, score_new, -1e+30)
        peak = jnp.maximum(lax.optimization_barrier(jnp.max(score_old, axis=-1)), lax.optimization_barrier(jnp.max(score_new, axis=-1)))
        weight_old = jnp.where(cache_mask, jnp.exp(score_old - peak[..., None]), 0.0)
        weight_new = jnp.where(new_mask, jnp.exp(score_new - peak[..., None]), 0.0)
        total = lax.optimization_barrier(jnp.sum(weight_old, axis=-1)) + lax.optimization_barrier(jnp.sum(weight_new, axis=-1))
        rounded_old = lax.optimization_barrier(weight_old.astype(jnp.bfloat16)).astype(jnp.float32)
        rounded_new = lax.optimization_barrier(weight_new.astype(jnp.bfloat16)).astype(jnp.float32)
        mixed = jnp.einsum('rhk,kd->rhd', rounded_old, value_old, preferred_element_type=jnp.float32)
        mixed = mixed + jnp.einsum('rhk,kd->rhd', rounded_new, value_new, preferred_element_type=jnp.float32)
        outputs.append(mixed)
        peaks.append(peak)
        totals.append(total)
    combined = jnp.concatenate(outputs, axis=1).reshape(query_rows, QUERY_HEADS * HEAD_DIMENSION)
    return (combined, jnp.concatenate(peaks, axis=1), jnp.concatenate(totals, axis=1))

def reference(queries, owners, new_keys, new_values, cache_keys, cache_values, lengths):
    tokens = slot_tokens(owners, N_CTX, TOKEN_SLOTS)
    query_rows = queries.shape[0]

    def visit(carry, device):
        best, acc_out, acc_sum = carry
        start = (device * CTX_DEV).astype(jnp.int32)
        slot_start = (device * TOKEN_SLOTS).astype(jnp.int32)
        keys = lax.dynamic_slice_in_dim(cache_keys, start, CTX_DEV)
        value_rows = lax.dynamic_slice_in_dim(cache_values, start, CTX_DEV)
        fresh_keys = lax.dynamic_slice_in_dim(new_keys, slot_start, TOKEN_SLOTS)
        fresh_values = lax.dynamic_slice_in_dim(new_values, slot_start, TOKEN_SLOTS)
        block_tokens = lax.dynamic_slice_in_dim(tokens, slot_start, TOKEN_SLOTS)
        live = lengths[device]
        output, peak, total = block_terms(queries, tokens, keys, value_rows, live, fresh_keys, fresh_values, block_tokens)
        merged = jnp.maximum(best, peak)
        older = jnp.exp(best - merged)
        newer = jnp.exp(peak - merged)
        acc_out = (acc_out.reshape(query_rows, QUERY_HEADS, HEAD_DIMENSION) * older[..., None] + output.reshape(query_rows, QUERY_HEADS, HEAD_DIMENSION) * newer[..., None]).reshape(query_rows, QUERY_HEADS * HEAD_DIMENSION)
        acc_sum = acc_sum * older + total * newer
        return ((merged, acc_out, acc_sum), None)
    start_state = (jnp.full((query_rows, QUERY_HEADS), -1e+30, jnp.float32), jnp.zeros((query_rows, QUERY_HEADS * HEAD_DIMENSION), jnp.float32), jnp.zeros((query_rows, QUERY_HEADS), jnp.float32))
    final_state, unused = lax.scan(visit, start_state, jnp.arange(N_CTX, dtype=jnp.int32))
    acc_out, acc_sum = (final_state[1], final_state[2])
    result = (acc_out.reshape(query_rows, QUERY_HEADS, HEAD_DIMENSION) / acc_sum[..., None]).reshape(query_rows, QUERY_HEADS * HEAD_DIMENSION)
    result = jnp.where(tokens[:, None] >= 0, result, 0.0)
    return result.astype(jnp.bfloat16)
```

```python
import math

import jax
import jax.numpy as jnp
from jax import lax
from jax.experimental import pallas as pl
from jax.experimental.pallas import tpu as pltpu
from jax.sharding import PartitionSpec as P

HEAD = 128
KV_HEADS = 8
SLOTS = 4
TOKENS = 256
KEYS = 256
DEVICES = 128
CHIP_MASKS = tuple((d >> 1) * 32 + (d & 1) * 2 for d in range(8))
PIECE = 2 * KEYS + 32
CHUNKS = 17
SCALE = math.log2(math.e) / math.sqrt(HEAD)
HIDDEN = -1e30


def swap(array, mask):
    return lax.ppermute(array, "ctx", [(i, i ^ mask) for i in range(DEVICES)])


def pack_kernel(head_ref, live_ref, queries, new_keys, new_values, keys, values, send, *rest):
    pieces, tail = rest[:8], rest[8]
    f32, bf16 = jnp.float32, jnp.bfloat16
    for y in range(4):
        for z in range(8):
            for low in range(4):
                at = (4 * y + low) * 256
                send[32 * y + 4 * z + low] = queries[:, at : at + 256]
    width = KV_HEADS * HEAD
    live = jnp.full((8, width), live_ref[0].astype(f32))
    gap = jnp.zeros((4, width), f32)
    tail[0:16, :] = jnp.concatenate([new_keys[...].astype(f32), gap, live], axis=0).astype(bf16)
    tail[16:32, :] = jnp.concatenate([new_values[...].astype(f32), gap, gap, gap], axis=0).astype(bf16)
    head = head_ref[0]
    for d in range(8):
        column = pl.ds(pl.multiple_of((head ^ d) * HEAD, HEAD), HEAD)
        pieces[d][0:KEYS, :] = keys[:, column]
        pieces[d][KEYS : 2 * KEYS, :] = values[:, column]
        pieces[d][2 * KEYS : PIECE, :] = tail[:, column]


def pack(head, live, queries, new_keys, new_values, keys, values):
    whole = pl.BlockSpec(memory_space=pltpu.VMEM)
    return pl.pallas_call(
        pack_kernel,
        out_shape=[jax.ShapeDtypeStruct((DEVICES, SLOTS, 256), jnp.bfloat16)]
        + [jax.ShapeDtypeStruct((PIECE, HEAD), jnp.bfloat16)] * 8,
        in_specs=[pl.BlockSpec(memory_space=pltpu.SMEM)] * 2 + [whole] * 5,
        out_specs=[whole] * 9,
        scratch_shapes=[pltpu.VMEM((32, KV_HEADS * HEAD), jnp.bfloat16)],
        cost_estimate=pl.CostEstimate(flops=0, bytes_accessed=2 << 20, transcendentals=0),
        name="pack",
    )(head, live, queries, new_keys, new_values, keys, values)


def attend_kernel(here_ref, q_ref, col_ref, row_ref, *rest):
    pieces, out_ref, scores, new_keys, new_values = rest[:16], rest[16], rest[17], rest[18], rest[19]
    f32, bf16, i32 = jnp.float32, jnp.bfloat16, jnp.int32
    here = here_ref[0]
    iota = lambda shape, dim: lax.broadcasted_iota(i32, shape, dim)
    own_col, own_row = col_ref[...], row_ref[...]

    same = own_col == own_row
    down, across = iota((TOKENS, TOKENS), 0), iota((TOKENS, TOKENS), 1)
    rank_col = jnp.sum(jnp.where(same & (across < down), 1.0, 0.0), axis=1, keepdims=True)
    rank_row = jnp.sum(jnp.where(same & (down < across), 1.0, 0.0), axis=0, keepdims=True)
    place_col = own_col * SLOTS + rank_col.astype(i32)
    place_row = own_row * SLOTS + rank_row.astype(i32)

    pick = jnp.where(place_col == iota((TOKENS, DEVICES * SLOTS), 1), 1.0, 0.0).astype(bf16)
    by_token = jnp.dot(pick, q_ref[...], preferred_element_type=f32).astype(bf16)
    queries = jnp.concatenate([by_token[:, :HEAD], by_token[:, HEAD:]], axis=0)

    contract = (((1,), (1,)), ((), ()))
    lane = iota((1, KEYS), 1).astype(f32)
    peak = jnp.full((2 * TOKENS, HEAD), HIDDEN, f32)
    for p in range(16):
        tail = pieces[p][2 * KEYS : 2 * KEYS + 16, :]
        new_keys[16 * p : 16 * p + 16, :] = tail
        new_values[16 * p : 16 * p + 16, :] = pieces[p][2 * KEYS + 16 : PIECE, :]
        live = tail.astype(f32)[8:9, 0:1]
        bias = jnp.where(lane < live, 0.0, HIDDEN)
        score = lax.dot_general(queries, pieces[p][0:KEYS, :], contract, preferred_element_type=f32)
        score = score * SCALE + bias
        scores[p] = score
        peak = jnp.maximum(peak, jnp.maximum(score[:, :HEAD], score[:, HEAD:]))

    column = iota((1, KEYS), 1)
    part, row = column >> 4, column & 15
    device = here ^ (((part >> 1) & 3) * 32 + (part & 1) * 2 + (part >> 3))
    slot = jnp.where(row < SLOTS, device * SLOTS + row, -1)
    match = place_col == slot
    token = jnp.sum(jnp.where(match, iota((TOKENS, KEYS), 0).astype(f32) + 1.0, 0.0), axis=0, keepdims=True) - 1.0
    reader = iota((2 * TOKENS, 1), 0)
    reader = jnp.where(reader >= TOKENS, reader - TOKENS, reader).astype(f32)
    seen = (token >= 0.0) & (token <= reader)
    score = lax.dot_general(queries, new_keys[...], contract, preferred_element_type=f32)
    score = jnp.where(seen, score * SCALE, HIDDEN)
    scores[16] = score
    peak = jnp.maximum(peak, jnp.maximum(score[:, :HEAD], score[:, HEAD:]))

    peak = jnp.max(peak, axis=1, keepdims=True)
    total = jnp.zeros((2 * TOKENS, HEAD), f32)
    mixed = jnp.zeros((2 * TOKENS, HEAD), f32)
    for p in range(CHUNKS):
        weight = jnp.exp2(scores[p] - peak)
        total = total + (weight[:, :HEAD] + weight[:, HEAD:])
        value = new_values[...] if p == 16 else pieces[p][KEYS : 2 * KEYS, :]
        mixed = mixed + jnp.dot(weight.astype(bf16), value, preferred_element_type=f32)
    total = jnp.sum(total, axis=1, keepdims=True)
    mean = mixed / total

    step = jnp.round(jnp.log2(jnp.maximum(jnp.max(jnp.abs(mean), axis=1, keepdims=True), 1e-30)))
    mean = mean * jnp.exp2(-step)
    rough = mean.astype(bf16)
    rest_of_mean = (mean - rough.astype(f32)).astype(bf16)
    level = peak + jnp.log2(total)
    high = level.astype(bf16).astype(f32)
    middle = (level - high).astype(bf16).astype(f32)
    low = level - high - middle
    lanes = iota((TOKENS, HEAD), 1)
    place = lanes & 63
    parts = jnp.zeros((TOKENS, HEAD), f32)
    for number, part in enumerate((high, middle, low, step)):
        parts = jnp.where(place == 2 * number, part[:TOKENS], parts)
        parts = jnp.where(place == 2 * number + 1, part[TOKENS:], parts)
    rows = jnp.concatenate(
        [rough[:TOKENS], rough[TOKENS:], rest_of_mean[:TOKENS], rest_of_mean[TOKENS:], parts.astype(bf16)],
        axis=1,
    )

    line = iota((TOKENS, TOKENS), 0) * 2
    even = jnp.where(line == place_row, 1.0, 0.0).astype(bf16)
    odd = jnp.where(line + 1 == place_row, 1.0, 0.0).astype(bf16)
    first = jnp.dot(even, rows, preferred_element_type=f32)
    second = jnp.dot(odd, rows, preferred_element_type=f32)
    out_ref[:, 0:256] = first[:, 0:256] + first[:, 256:512]
    out_ref[:, 256:512] = second[:, 0:256] + second[:, 256:512]
    out_ref[:, 512:640] = jnp.where(lanes < 64, first[:, 512:], second[:, 512:])


def attend(here, queries, own_col, own_row, pieces):
    whole = pl.BlockSpec(memory_space=pltpu.VMEM)
    return pl.pallas_call(
        attend_kernel,
        out_shape=jax.ShapeDtypeStruct((TOKENS, 640), jnp.float32),
        in_specs=[pl.BlockSpec(memory_space=pltpu.SMEM)] + [whole] * 19,
        out_specs=whole,
        scratch_shapes=[
            pltpu.VMEM((CHUNKS, 2 * TOKENS, KEYS), jnp.float32),
            pltpu.VMEM((KEYS, HEAD), jnp.bfloat16),
            pltpu.VMEM((KEYS, HEAD), jnp.bfloat16),
        ],
        compiler_params=pltpu.CompilerParams(vmem_limit_bytes=40 << 20),
        cost_estimate=pl.CostEstimate(
            flops=4 * 512 * 4352 * 128, bytes_accessed=3 << 20, transcendentals=512 * 4352
        ),
        name="attend",
    )(here, queries, own_col, own_row, *pieces)


def combine_kernel(parts_ref, out_ref):
    rows = parts_ref[...]
    levels = rows[:, 512:640]
    for v in range(4):
        at = 64 * (v // 2) + v % 2
        level = levels[:, at : at + 1] + levels[:, at + 2 : at + 3] + levels[:, at + 4 : at + 5]
        level = level.reshape(4, 8, 8, 1)
        factor = jnp.exp2(level - jnp.max(level, axis=1, keepdims=True))
        step = jnp.exp2(levels[:, at + 6 : at + 7]).reshape(4, 8, 8, 1)
        mean = rows[:, v * HEAD : (v + 1) * HEAD].reshape(4, 8, 8, HEAD)
        whole = jnp.sum(mean * (factor * step), axis=1) / jnp.sum(factor, axis=1)
        out_ref[:, v * HEAD : (v + 1) * HEAD] = whole.reshape(32, HEAD)


def combine(parts):
    whole = pl.BlockSpec(memory_space=pltpu.VMEM)
    return pl.pallas_call(
        combine_kernel,
        out_shape=jax.ShapeDtypeStruct((32, 512), jnp.float32),
        in_specs=[whole],
        out_specs=whole,
        name="combine",
    )(parts)


def per_device(queries, owners, new_keys, new_values, cache_keys, cache_values, lengths):
    bf16 = jnp.bfloat16
    here = lax.axis_index("ctx").astype(jnp.int32)
    head = (here >> 5) * 2 + ((here >> 1) & 1)

    send, *mine = pack(head[None], lengths, queries, new_keys, new_values, cache_keys, cache_values)
    everyone = lax.all_to_all(send, "ctx", 0, 0).reshape(DEVICES * SLOTS, 256)
    held = [mine[0]] + [swap(mine[d], CHIP_MASKS[d]) for d in range(1, 8)]
    other = [swap(piece, 1) for piece in held]

    partial = attend(here[None], everyone, owners, owners.reshape(1, TOKENS), held + other)
    spread = lax.all_to_all(partial.astype(jnp.float16).reshape(DEVICES, 2, 640), "ctx", 0, 0)
    result = combine(spread.astype(jnp.float32).reshape(2 * DEVICES, 640))
    result = result.reshape(16, 2, 2, 256).transpose(1, 2, 0, 3).reshape(SLOTS, 4096)
    return result.astype(bf16)


def solution(mesh):
    return jax.shard_map(
        per_device,
        mesh=mesh,
        in_specs=(
            P(("batch", "ctx"), None),
            P("batch", None),
            P(("batch", "ctx"), None),
            P(("batch", "ctx"), None),
            P(("batch", "ctx"), None),
            P(("batch", "ctx"), None),
            P(("batch", "ctx")),
        ),
        out_specs=P(("batch", "ctx"), None),
        check_vma=False,
    )
```

```python
import math

import jax
import jax.numpy as jnp
from jax import lax
from jax.experimental import pallas as pl
from jax.experimental.pallas import tpu as pltpu
from jax.sharding import PartitionSpec as P

HEAD = 128
KV_HEADS = 8
SLOTS = 4
TOKENS = 256
KEYS = 256
DEVICES = 128
CHIP_MASKS = tuple((d >> 2) * 32 + (d >> 1 & 1) * 4 + (d & 1) * 2 for d in range(8))
ORDER = (0, 7, 6, 5, 3, 4, 2, 1)
EARLY = 4
AFTER = (0, 0, 0, 0, 0, 1, 2, 3)
PREPARE_FLOPS = 2850000000
PACK_LIMIT = 60
PIECE = 2 * KEYS + 32
CHUNKS = 17
BLOCK = 128
SCALE = math.log2(math.e) / math.sqrt(HEAD)
HIDDEN = -1e30


def swap(array, mask):
    return lax.ppermute(array, "ctx", [(i, i ^ mask) for i in range(DEVICES)])


def pack_kernel(head_ref, live_ref, *rest):
    given, send, pieces, tail, held, sems = rest[:5], rest[5], rest[6:14], rest[14], rest[15:20], rest[20]
    f32, bf16 = jnp.float32, jnp.bfloat16
    fetches = [pltpu.make_async_copy(given[i], held[i], sems.at[i]) for i in range(5)]
    for fetch in fetches:
        fetch.start()
    queries, new_keys, new_values, keys, values = held
    fetches[0].wait()
    for device in range(DEVICES):
        at = ((device >> 5 & 1) * 8 + (device >> 2 & 1) * 4 + (device & 3)) * 256
        send[device] = queries[:, at : at + 256]
    width = KV_HEADS * HEAD
    fetches[1].wait()
    fetches[2].wait()
    live = jnp.full((8, width), live_ref[0].astype(f32))
    gap = jnp.zeros((4, width), f32)
    tail[0:16, :] = jnp.concatenate([new_keys[...].astype(f32), gap, live], axis=0).astype(bf16)
    tail[16:32, :] = jnp.concatenate([new_values[...].astype(f32), gap, gap, gap], axis=0).astype(bf16)
    head = head_ref[0]
    columns = [pl.ds(pl.multiple_of((head ^ d) * HEAD, HEAD), HEAD) for d in range(8)]
    for d in range(8):
        pieces[d][2 * KEYS : PIECE, :] = tail[:, columns[d]]
    fetches[3].wait()
    for d in range(8):
        pieces[d][0:KEYS, :] = keys[:, columns[d]]
    fetches[4].wait()
    for d in range(8):
        pieces[d][KEYS : 2 * KEYS, :] = values[:, columns[d]]


def pack(head, live, queries, new_keys, new_values, keys, values):
    whole = pl.BlockSpec(memory_space=pltpu.VMEM)
    return pl.pallas_call(
        pack_kernel,
        out_shape=[jax.ShapeDtypeStruct((DEVICES, SLOTS, 256), jnp.bfloat16)]
        + [jax.ShapeDtypeStruct((PIECE, HEAD), jnp.bfloat16)] * 8,
        in_specs=[pl.BlockSpec(memory_space=pltpu.SMEM)] * 2
        + [pl.BlockSpec(memory_space=pl.ANY)] * 5,
        out_specs=[whole] * 9,
        scratch_shapes=[
            pltpu.VMEM((32, KV_HEADS * HEAD), jnp.bfloat16),
            pltpu.VMEM((SLOTS, 4096), jnp.bfloat16),
            pltpu.VMEM((SLOTS, KV_HEADS * HEAD), jnp.bfloat16),
            pltpu.VMEM((SLOTS, KV_HEADS * HEAD), jnp.bfloat16),
            pltpu.VMEM((KEYS, KV_HEADS * HEAD), jnp.bfloat16),
            pltpu.VMEM((KEYS, KV_HEADS * HEAD), jnp.bfloat16),
            pltpu.SemaphoreType.DMA((5,)),
        ],
        compiler_params=pltpu.CompilerParams(vmem_limit_bytes=PACK_LIMIT << 20),
        cost_estimate=pl.CostEstimate(flops=0, bytes_accessed=2 << 20, transcendentals=0),
        name="pack",
    )(head, live, queries, new_keys, new_values, keys, values)


def prepare_kernel(here_ref, col_ref, row_ref, *rest):
    pieces, (pick, near, far, token_ref, tails) = rest[:EARLY], rest[EARLY:]
    f32, bf16, i32 = jnp.float32, jnp.bfloat16, jnp.int32
    here = here_ref[0]
    iota = lambda shape, dim: lax.broadcasted_iota(i32, shape, dim)
    own_col, own_row = col_ref[...], row_ref[...]

    same = own_col == own_row
    down, across = iota((TOKENS, TOKENS), 0), iota((TOKENS, TOKENS), 1)
    rank_col = jnp.sum(jnp.where(same & (across < down), 1.0, 0.0), axis=1, keepdims=True)
    rank_row = jnp.sum(jnp.where(same & (down < across), 1.0, 0.0), axis=0, keepdims=True)
    place_col = own_col * SLOTS + rank_col.astype(i32)
    place_row = own_row * SLOTS + rank_row.astype(i32)

    pick[...] = jnp.where(place_col == iota((TOKENS, DEVICES * SLOTS), 1), 1.0, 0.0).astype(bf16)
    line = (down >> 1) * SLOTS + (down & 1)
    near[...] = jnp.where(line == place_row, 1.0, 0.0).astype(bf16)
    far[...] = jnp.where(line + 2 == place_row, 1.0, 0.0).astype(bf16)

    column = iota((1, KEYS), 1)
    part, row = column >> 4, column & 15
    chip = jnp.zeros_like(part)
    for number, d in enumerate(ORDER):
        chip = jnp.where((part & 7) == number, CHIP_MASKS[d], chip)
    device = here ^ (chip + (part >> 3))
    slot = jnp.where(row < SLOTS, device * SLOTS + row, -1)
    token = jnp.where(place_col == slot, down.astype(f32) + 1.0, 0.0)
    token_ref[...] = jnp.sum(token, axis=0, keepdims=True) - 1.0

    for p in range(EARLY):
        tails[32 * p : 32 * p + 32, :] = pieces[p][2 * KEYS : PIECE, :]


def prepare(here, own_col, own_row, pieces):
    whole = pl.BlockSpec(memory_space=pltpu.VMEM)
    shape = jax.ShapeDtypeStruct
    return pl.pallas_call(
        prepare_kernel,
        out_shape=[
            shape((TOKENS, DEVICES * SLOTS), jnp.bfloat16),
            shape((TOKENS, TOKENS), jnp.bfloat16),
            shape((TOKENS, TOKENS), jnp.bfloat16),
            shape((1, KEYS), jnp.float32),
            shape((32 * EARLY, HEAD), jnp.bfloat16),
        ],
        in_specs=[pl.BlockSpec(memory_space=pltpu.SMEM)] + [whole] * (2 + EARLY),
        out_specs=[whole] * 5,
        compiler_params=pltpu.CompilerParams(vmem_limit_bytes=8 << 20),
        cost_estimate=pl.CostEstimate(flops=PREPARE_FLOPS, bytes_accessed=1 << 19, transcendentals=0),
        name="prepare",
    )(here, own_col, own_row, *pieces)


def attend_kernel(q_ref, pick, near, far, token_ref, tails, *rest):
    pieces, out_ref = rest[:16], rest[16]
    scores, bias, new_keys, new_values = rest[17:]
    f32, bf16 = jnp.float32, jnp.bfloat16
    iota = lambda shape, dim: lax.broadcasted_iota(jnp.int32, shape, dim)

    by_token = jnp.dot(pick[...], q_ref[...], preferred_element_type=f32).astype(bf16)
    first_lane = jnp.where(iota((BLOCK, HEAD), 1) == 0, 1.0, 0.0).astype(bf16)

    key_row = iota((KEYS, HEAD), 0).astype(f32)
    for p in range(16):
        tail = pieces[p][2 * KEYS : PIECE, :] if p >= EARLY else tails[32 * p : 32 * p + 32, :]
        new_keys[16 * p : 16 * p + 16, :] = tail[0:16]
        new_values[16 * p : 16 * p + 16, :] = tail[16:32]
        live = tail[0:16].astype(f32)[8:9, 0:1]
        bias[p] = jnp.where(key_row < live, 0.0, HIDDEN).astype(bf16)

    token = token_ref[...]
    contract = (((1,), (1,)), ((), ()))
    lanes = iota((BLOCK, HEAD), 1)
    place = lanes & 63
    rows = []
    for b in range(4):
        head, start = b // 2, b % 2 * BLOCK
        plain = by_token[start : start + BLOCK, head * HEAD : (head + 1) * HEAD]
        query = jnp.concatenate([plain, first_lane], axis=1)
        peak = jnp.full((BLOCK, HEAD), HIDDEN, f32)
        for p in range(16):
            key = jnp.concatenate([pieces[p][0:KEYS, :], bias[p]], axis=1)
            score = lax.dot_general(query, key, contract, preferred_element_type=f32)
            scores[b, p] = score
            peak = jnp.maximum(peak, jnp.maximum(score[:, :HEAD], score[:, HEAD:]))
        reader = (iota((BLOCK, 1), 0) + start).astype(f32)
        seen = (token >= 0.0) & (token <= reader)
        score = lax.dot_general(plain, new_keys[...], contract, preferred_element_type=f32)
        score = jnp.where(seen, score, HIDDEN)
        scores[b, 16] = score
        peak = jnp.maximum(peak, jnp.maximum(score[:, :HEAD], score[:, HEAD:]))
        peak = jnp.max(peak, axis=1, keepdims=True)

        total = jnp.zeros((BLOCK, HEAD), f32)
        mixed = jnp.zeros((BLOCK, HEAD), f32)
        for p in range(CHUNKS):
            weight = jnp.exp2((scores[b, p] - peak) * SCALE)
            total = total + (weight[:, :HEAD] + weight[:, HEAD:])
            value = new_values[...] if p == 16 else pieces[p][KEYS : 2 * KEYS, :]
            mixed = mixed + jnp.dot(weight.astype(bf16), value, preferred_element_type=f32)
        total = jnp.sum(total, axis=1, keepdims=True)
        mean = mixed / total

        reach = jnp.max(jnp.abs(mean), axis=1, keepdims=True)
        step = jnp.round(jnp.log2(jnp.maximum(reach, 1e-30)))
        mean = mean * jnp.exp2(-step)
        rough = mean.astype(bf16)
        fine = (mean - rough.astype(f32)).astype(bf16)
        level = peak * SCALE + jnp.log2(total)
        high = level.astype(bf16).astype(f32)
        middle = (level - high).astype(bf16).astype(f32)
        low = level - high - middle
        parts = jnp.zeros((BLOCK, HEAD), f32)
        for number, value in enumerate((high, middle, low, step)):
            parts = jnp.where(place == 2 * number + head, value, parts)
        rows.append((rough, fine, parts))

    whole = jnp.concatenate(
        [
            jnp.concatenate([rows[h][0], rows[h + 2][0], rows[h][1], rows[h + 2][1], (rows[h][2] + rows[h + 2][2]).astype(bf16)], axis=1)
            for h in range(2)
        ],
        axis=0,
    )

    first = jnp.dot(near[...], whole, preferred_element_type=f32)
    second = jnp.dot(far[...], whole, preferred_element_type=f32)
    out_ref[:, 0:256] = first[:, 0:256] + first[:, 256:512]
    out_ref[:, 256:512] = second[:, 0:256] + second[:, 256:512]
    out_ref[:, 512:640] = jnp.where(iota((TOKENS, HEAD), 1) < 64, first[:, 512:], second[:, 512:])


def attend(queries, prepared, pieces):
    whole = pl.BlockSpec(memory_space=pltpu.VMEM)
    return pl.pallas_call(
        attend_kernel,
        out_shape=jax.ShapeDtypeStruct((TOKENS, 640), jnp.float32),
        in_specs=[whole] * 22,
        out_specs=whole,
        scratch_shapes=[
            pltpu.VMEM((4, CHUNKS, BLOCK, KEYS), jnp.float32),
            pltpu.VMEM((16, KEYS, HEAD), jnp.bfloat16),
            pltpu.VMEM((KEYS, HEAD), jnp.bfloat16),
            pltpu.VMEM((KEYS, HEAD), jnp.bfloat16),
        ],
        compiler_params=pltpu.CompilerParams(vmem_limit_bytes=20 << 20),
        cost_estimate=pl.CostEstimate(
            flops=4 * 512 * 4352 * 128, bytes_accessed=3 << 20, transcendentals=512 * 4352
        ),
        name="attend",
    )(queries, *prepared, *pieces)


def combine_kernel(parts_ref, out_ref, whole):
    split = lambda array: array.reshape(2, 2, 4, 8, 2, array.shape[-1])
    levels = parts_ref[:, :, 512:640]
    ahead = lambda count: pltpu.roll(levels, HEAD - count, 2)
    step = jnp.exp2(ahead(6))
    level = split(levels + ahead(2) + ahead(4))
    factor = jnp.exp2(level - jnp.max(level, axis=(0, 2), keepdims=True))
    factor = factor / jnp.sum(factor, axis=(0, 2), keepdims=True) * split(step)
    for v in range(4):
        at = 64 * (v // 2) + v % 2
        mean = split(parts_ref[:, :, v * HEAD : (v + 1) * HEAD])
        mean = jnp.sum(mean * factor[..., at : at + 1], axis=(0, 2)).reshape(16, 2, HEAD)
        for pair in range(16):
            column = pair * 256 + v % 2 * HEAD
            whole[v // 2 * 2 : v // 2 * 2 + 2, column : column + HEAD] = mean[pair]
    out_ref[...] = whole[...].astype(jnp.bfloat16)


def combine(parts):
    whole = pl.BlockSpec(memory_space=pltpu.VMEM)
    return pl.pallas_call(
        combine_kernel,
        out_shape=jax.ShapeDtypeStruct((SLOTS, 4096), jnp.bfloat16),
        in_specs=[whole],
        out_specs=whole,
        scratch_shapes=[pltpu.VMEM((SLOTS, 4096), jnp.float32)],
        compiler_params=pltpu.CompilerParams(vmem_limit_bytes=16 << 20),
        name="combine",
    )(parts)


def per_device(queries, owners, new_keys, new_values, cache_keys, cache_values, lengths):
    bf16 = jnp.bfloat16
    here = lax.axis_index("ctx").astype(jnp.int32)
    head = (here >> 5 & 1) * 4 + (here >> 2 & 1) * 2 + (here >> 1 & 1)

    send, *mine = pack(head[None], lengths, queries, new_keys, new_values, cache_keys, cache_values)
    held = [mine[0]]
    for number, d in enumerate(ORDER[1:], 1):
        piece = mine[d]
        if AFTER[number]:
            piece, _ = lax.optimization_barrier((piece, held[AFTER[number]]))
        held.append(swap(piece, CHIP_MASKS[d]))
    other = [swap(piece, 1) for piece in held]
    everyone = lax.all_to_all(send, "ctx", 0, 0).reshape(DEVICES * SLOTS, 256)
    prepared = prepare(here[None], owners, owners.reshape(1, TOKENS), held[:EARLY])
    partial = attend(everyone, prepared, held + other)
    partial = partial.astype(jnp.float16).reshape(DEVICES, 2, 640)
    return combine(lax.all_to_all(partial, "ctx", 0, 0).astype(jnp.float32))


def solution(mesh):
    return jax.shard_map(
        per_device,
        mesh=mesh,
        in_specs=(
            P(("batch", "ctx"), None),
            P("batch", None),
            P(("batch", "ctx"), None),
            P(("batch", "ctx"), None),
            P(("batch", "ctx"), None),
            P(("batch", "ctx"), None),
            P(("batch", "ctx")),
        ),
        out_specs=P(("batch", "ctx"), None),
        check_vma=False,
    )
```

```python
import math

import jax
import jax.numpy as jnp
from jax import lax
from jax.experimental import pallas as pl
from jax.experimental.pallas import tpu as pltpu
from jax.sharding import PartitionSpec as P

HEAD = 128
KV_HEADS = 8
SLOTS = 4
TOKENS = 256
KEYS = 256
DEVICES = 128
CHIP_MASKS = tuple((d >> 2) * 32 + (d >> 1 & 1) * 4 + (d & 1) * 2 for d in range(8))
ORDER = (0, 6, 5, 7, 3, 1, 4, 2)
EARLY = 4
AFTER = (0, 0, 0, 0, 0, 2, 3, 4)
PREPARE_FLOPS = 2850000000
PACK_LIMIT = 60
PIECE = 2 * KEYS + 32
CHUNKS = 17
BLOCK = 256
SCALE = math.log2(math.e) / math.sqrt(HEAD)
HIDDEN = -1e30


def swap(array, mask):
    return lax.ppermute(array, "ctx", [(i, i ^ mask) for i in range(DEVICES)])


def pack_kernel(head_ref, live_ref, *rest):
    given, send, pieces, tail, held, sems = rest[:5], rest[5], rest[6:14], rest[14], rest[15:20], rest[20]
    f32, bf16 = jnp.float32, jnp.bfloat16
    fetches = [pltpu.make_async_copy(given[i], held[i], sems.at[i]) for i in range(5)]
    for fetch in fetches:
        fetch.start()
    queries, new_keys, new_values, keys, values = held
    fetches[0].wait()
    for device in range(DEVICES):
        at = ((device >> 5 & 1) * 8 + (device >> 2 & 1) * 4 + (device & 3)) * 256
        send[device] = queries[:, at : at + 256]
    width = KV_HEADS * HEAD
    fetches[1].wait()
    fetches[2].wait()
    live = jnp.full((8, width), live_ref[0].astype(f32))
    gap = jnp.zeros((4, width), f32)
    tail[0:16, :] = jnp.concatenate([new_keys[...].astype(f32), gap, live], axis=0).astype(bf16)
    tail[16:32, :] = jnp.concatenate([new_values[...].astype(f32), gap, gap, gap], axis=0).astype(bf16)
    head = head_ref[0]
    columns = [pl.ds(pl.multiple_of((head ^ d) * HEAD, HEAD), HEAD) for d in range(8)]
    for d in range(8):
        pieces[d][2 * KEYS : PIECE, :] = tail[:, columns[d]]
    fetches[3].wait()
    for d in range(8):
        pieces[d][0:KEYS, :] = keys[:, columns[d]]
    fetches[4].wait()
    for d in range(8):
        pieces[d][KEYS : 2 * KEYS, :] = values[:, columns[d]]


def pack(head, live, queries, new_keys, new_values, keys, values):
    whole = pl.BlockSpec(memory_space=pltpu.VMEM)
    return pl.pallas_call(
        pack_kernel,
        out_shape=[jax.ShapeDtypeStruct((DEVICES, SLOTS, 256), jnp.bfloat16)]
        + [jax.ShapeDtypeStruct((PIECE, HEAD), jnp.bfloat16)] * 8,
        in_specs=[pl.BlockSpec(memory_space=pltpu.SMEM)] * 2
        + [pl.BlockSpec(memory_space=pltpu.HBM)] * 5,
        out_specs=[whole] * 9,
        scratch_shapes=[
            pltpu.VMEM((32, KV_HEADS * HEAD), jnp.bfloat16),
            pltpu.VMEM((SLOTS, 4096), jnp.bfloat16),
            pltpu.VMEM((SLOTS, KV_HEADS * HEAD), jnp.bfloat16),
            pltpu.VMEM((SLOTS, KV_HEADS * HEAD), jnp.bfloat16),
            pltpu.VMEM((KEYS, KV_HEADS * HEAD), jnp.bfloat16),
            pltpu.VMEM((KEYS, KV_HEADS * HEAD), jnp.bfloat16),
            pltpu.SemaphoreType.DMA((5,)),
        ],
        compiler_params=pltpu.CompilerParams(vmem_limit_bytes=PACK_LIMIT << 20),
        cost_estimate=pl.CostEstimate(flops=0, bytes_accessed=2 << 20, transcendentals=0),
        name="pack",
    )(head, live, queries, new_keys, new_values, keys, values)


def prepare_kernel(here_ref, col_ref, row_ref, *rest):
    pieces, (pick, near, far, token_ref, tails) = rest[:EARLY], rest[EARLY:]
    f32, bf16, i32 = jnp.float32, jnp.bfloat16, jnp.int32
    here = here_ref[0]
    iota = lambda shape, dim: lax.broadcasted_iota(i32, shape, dim)
    own_col, own_row = col_ref[...], row_ref[...]

    same = own_col == own_row
    down, across = iota((TOKENS, TOKENS), 0), iota((TOKENS, TOKENS), 1)
    rank_col = jnp.sum(jnp.where(same & (across < down), 1.0, 0.0), axis=1, keepdims=True)
    rank_row = jnp.sum(jnp.where(same & (down < across), 1.0, 0.0), axis=0, keepdims=True)
    place_col = own_col * SLOTS + rank_col.astype(i32)
    place_row = own_row * SLOTS + rank_row.astype(i32)

    pick[...] = jnp.where(place_col == iota((TOKENS, DEVICES * SLOTS), 1), 1.0, 0.0).astype(bf16)
    line = (down >> 1) * SLOTS + (down & 1)
    near[...] = jnp.where(line == place_row, 1.0, 0.0).astype(bf16)
    far[...] = jnp.where(line + 2 == place_row, 1.0, 0.0).astype(bf16)

    column = iota((1, KEYS), 1)
    part, row = column >> 4, column & 15
    chip = jnp.zeros_like(part)
    for number, d in enumerate(ORDER):
        chip = jnp.where((part & 7) == number, CHIP_MASKS[d], chip)
    device = here ^ (chip + (part >> 3))
    slot = jnp.where(row < SLOTS, device * SLOTS + row, -1)
    token = jnp.where(place_col == slot, down.astype(f32) + 1.0, 0.0)
    token_ref[...] = jnp.sum(token, axis=0, keepdims=True) - 1.0

    for p in range(EARLY):
        tails[32 * p : 32 * p + 32, :] = pieces[p][2 * KEYS : PIECE, :]


def prepare(here, own_col, own_row, pieces):
    whole = pl.BlockSpec(memory_space=pltpu.VMEM)
    shape = jax.ShapeDtypeStruct
    return pl.pallas_call(
        prepare_kernel,
        out_shape=[
            shape((TOKENS, DEVICES * SLOTS), jnp.bfloat16),
            shape((TOKENS, TOKENS), jnp.bfloat16),
            shape((TOKENS, TOKENS), jnp.bfloat16),
            shape((1, KEYS), jnp.float32),
            shape((32 * EARLY, HEAD), jnp.bfloat16),
        ],
        in_specs=[pl.BlockSpec(memory_space=pltpu.SMEM)] + [whole] * (2 + EARLY),
        out_specs=[whole] * 5,
        compiler_params=pltpu.CompilerParams(vmem_limit_bytes=8 << 20),
        cost_estimate=pl.CostEstimate(flops=PREPARE_FLOPS, bytes_accessed=1 << 19, transcendentals=0),
        name="prepare",
    )(here, own_col, own_row, *pieces)


def attend_kernel(q_ref, pick, near, far, token_ref, tails, *rest):
    pieces, out_ref = rest[:16], rest[16]
    scores, new_keys, new_values = rest[17:]
    f32, bf16 = jnp.float32, jnp.bfloat16
    iota = lambda shape, dim: lax.broadcasted_iota(jnp.int32, shape, dim)

    by_token = jnp.dot(pick[...], q_ref[...], preferred_element_type=f32).astype(bf16)

    lane_bias = []
    for p in range(16):
        tail = pieces[p][2 * KEYS : PIECE, :] if p >= EARLY else tails[32 * p : 32 * p + 32, :]
        new_keys[16 * p : 16 * p + 16, :] = tail[0:16]
        new_values[16 * p : 16 * p + 16, :] = tail[16:32]
        live = tail[0:16].astype(f32)[8:9, 0:1]
        lane_bias.append(jnp.where(iota((1, KEYS), 1).astype(f32) < live, 0.0, HIDDEN))

    token = token_ref[...]
    contract = (((1,), (1,)), ((), ()))
    peaks = []
    for b in range(2):
        head, start = b, 0
        plain = by_token[start : start + BLOCK, head * HEAD : (head + 1) * HEAD]
        peak = jnp.full((BLOCK, HEAD), HIDDEN, f32)
        for p in range(16):
            score = lax.dot_general(
                plain, pieces[p][0:KEYS, :], contract, preferred_element_type=f32
            )
            score = score + lane_bias[p]
            scores[b, p] = score
            peak = jnp.maximum(peak, jnp.maximum(score[:, :HEAD], score[:, HEAD:]))
        reader = (iota((BLOCK, 1), 0) + start).astype(f32)
        seen = (token >= 0.0) & (token <= reader)
        score = lax.dot_general(plain, new_keys[...], contract, preferred_element_type=f32)
        score = jnp.where(seen, score, HIDDEN)
        scores[b, 16] = score
        peak = jnp.maximum(peak, jnp.maximum(score[:, :HEAD], score[:, HEAD:]))
        peaks.append(jnp.max(peak, axis=1, keepdims=True))

    totals, sums = [], []
    for b in range(2):
        total = jnp.zeros((BLOCK, HEAD), f32)
        mixed = jnp.zeros((BLOCK, HEAD), f32)
        for p in range(CHUNKS):
            weight = jnp.exp2((scores[b, p] - peaks[b]) * SCALE)
            total = total + (weight[:, :HEAD] + weight[:, HEAD:])
            value = new_values[...] if p == 16 else pieces[p][KEYS : 2 * KEYS, :]
            mixed = mixed + jnp.dot(weight.astype(bf16), value, preferred_element_type=f32)
        totals.append(jnp.sum(total, axis=1, keepdims=True))
        sums.append(mixed)
    peak, total = jnp.concatenate(peaks, axis=0), jnp.concatenate(totals, axis=0)
    mean = jnp.concatenate(sums, axis=0) / total

    reach = jnp.max(jnp.abs(mean), axis=1, keepdims=True)
    step = jnp.round(jnp.log2(jnp.maximum(reach, 1e-30)))
    mean = mean * jnp.exp2(-step)
    rough = mean.astype(bf16)
    fine = (mean - rough.astype(f32)).astype(bf16)
    level = peak * SCALE + jnp.log2(total)
    high = level.astype(bf16).astype(f32)
    middle = (level - high).astype(bf16).astype(f32)
    low = level - high - middle
    place = iota((TOKENS, HEAD), 1) & 63
    parts = jnp.zeros((TOKENS, HEAD), f32)
    for number, value in enumerate((high, middle, low, step)):
        parts = jnp.where(place == 2 * number, value[:TOKENS], parts)
        parts = jnp.where(place == 2 * number + 1, value[TOKENS:], parts)
    whole = jnp.concatenate(
        [rough[:TOKENS], rough[TOKENS:], fine[:TOKENS], fine[TOKENS:], parts.astype(bf16)], axis=1
    )

    first = jnp.dot(near[...], whole, preferred_element_type=f32)
    second = jnp.dot(far[...], whole, preferred_element_type=f32)
    out_ref[:, 0:256] = first[:, 0:256] + first[:, 256:512]
    out_ref[:, 256:512] = second[:, 0:256] + second[:, 256:512]
    out_ref[:, 512:640] = jnp.where(iota((TOKENS, HEAD), 1) < 64, first[:, 512:], second[:, 512:])


def attend(queries, prepared, pieces):
    whole = pl.BlockSpec(memory_space=pltpu.VMEM)
    return pl.pallas_call(
        attend_kernel,
        out_shape=jax.ShapeDtypeStruct((TOKENS, 640), jnp.float32),
        in_specs=[whole] * 22,
        out_specs=whole,
        scratch_shapes=[
            pltpu.VMEM((2, CHUNKS, BLOCK, KEYS), jnp.float32),
            pltpu.VMEM((KEYS, HEAD), jnp.bfloat16),
            pltpu.VMEM((KEYS, HEAD), jnp.bfloat16),
        ],
        compiler_params=pltpu.CompilerParams(vmem_limit_bytes=20 << 20),
        cost_estimate=pl.CostEstimate(
            flops=4 * 512 * 4352 * 128, bytes_accessed=3 << 20, transcendentals=512 * 4352
        ),
        name="attend",
    )(queries, *prepared, *pieces)


def combine_kernel(parts_ref, out_ref, whole):
    split = lambda array: array.reshape(2, 2, 4, 8, 2, array.shape[-1])
    levels = parts_ref[:, :, 512:640]
    ahead = lambda count: pltpu.roll(levels, HEAD - count, 2)
    step = jnp.exp2(ahead(6))
    level = split(levels + ahead(2) + ahead(4))
    factor = jnp.exp2(level - jnp.max(level, axis=(0, 2), keepdims=True))
    factor = factor / jnp.sum(factor, axis=(0, 2), keepdims=True) * split(step)
    for v in range(4):
        at = 64 * (v // 2) + v % 2
        mean = split(parts_ref[:, :, v * HEAD : (v + 1) * HEAD])
        mean = jnp.sum(mean * factor[..., at : at + 1], axis=(0, 2)).reshape(16, 2, HEAD)
        for pair in range(16):
            column = pair * 256 + v % 2 * HEAD
            whole[v // 2 * 2 : v // 2 * 2 + 2, column : column + HEAD] = mean[pair]
    out_ref[...] = whole[...].astype(jnp.bfloat16)


def combine(parts):
    whole = pl.BlockSpec(memory_space=pltpu.VMEM)
    return pl.pallas_call(
        combine_kernel,
        out_shape=jax.ShapeDtypeStruct((SLOTS, 4096), jnp.bfloat16),
        in_specs=[whole],
        out_specs=whole,
        scratch_shapes=[pltpu.VMEM((SLOTS, 4096), jnp.float32)],
        compiler_params=pltpu.CompilerParams(vmem_limit_bytes=16 << 20),
        name="combine",
    )(parts)


def per_device(queries, owners, new_keys, new_values, cache_keys, cache_values, lengths):
    bf16 = jnp.bfloat16
    here = lax.axis_index("ctx").astype(jnp.int32)
    head = (here >> 5 & 1) * 4 + (here >> 2 & 1) * 2 + (here >> 1 & 1)

    send, *mine = pack(head[None], lengths, queries, new_keys, new_values, cache_keys, cache_values)
    held = [mine[0]]
    for number, d in enumerate(ORDER[1:], 1):
        piece = mine[d]
        if AFTER[number]:
            piece, _ = lax.optimization_barrier((piece, held[AFTER[number]]))
        held.append(swap(piece, CHIP_MASKS[d]))
    other = [swap(piece, 1) for piece in held]
    everyone = lax.all_to_all(send, "ctx", 0, 0).reshape(DEVICES * SLOTS, 256)
    prepared = prepare(here[None], owners, owners.reshape(1, TOKENS), held[:EARLY])
    partial = attend(everyone, prepared, held + other)
    partial = partial.astype(jnp.float16).reshape(DEVICES, 2, 640)
    return combine(lax.all_to_all(partial, "ctx", 0, 0).astype(jnp.float32))


def solution(mesh):
    return jax.shard_map(
        per_device,
        mesh=mesh,
        in_specs=(
            P(("batch", "ctx"), None),
            P("batch", None),
            P(("batch", "ctx"), None),
            P(("batch", "ctx"), None),
            P(("batch", "ctx"), None),
            P(("batch", "ctx"), None),
            P(("batch", "ctx")),
        ),
        out_specs=P(("batch", "ctx"), None),
        check_vma=False,
    )
```

```python
import math

import jax
import jax.numpy as jnp
from jax import lax
from jax.experimental import pallas as pl
from jax.experimental.pallas import tpu as pltpu
from jax.sharding import PartitionSpec as P

HEAD = 128
KV_HEADS = 8
SLOTS = 4
TOKENS = 256
KEYS = 256
DEVICES = 128
CHIP_MASKS = tuple((d >> 1) * 32 + (d & 1) * 2 for d in range(8))
ORDER = (0, 7, 3, 5, 4, 1, 6, 2)
EARLY = 4
AFTER = (0, 0, 0, 0, 0, 2, 3, 4)
PREPARE_FLOPS = 2850000000
PACK_LIMIT = 56
PIECE = 2 * KEYS + 32
CHUNKS = 17
BLOCK = 256
SCALE = math.log2(math.e) / math.sqrt(HEAD)
HIDDEN = -1e30


def swap(array, mask):
    return lax.ppermute(array, "ctx", [(i, i ^ mask) for i in range(DEVICES)])


def pack_kernel(head_ref, live_ref, *rest):
    given, send, pieces, tail, held, sems = rest[:5], rest[5], rest[6:14], rest[14], rest[15:20], rest[20]
    f32, bf16 = jnp.float32, jnp.bfloat16
    fetches = [pltpu.make_async_copy(given[i], held[i], sems.at[i]) for i in range(5)]
    for fetch in fetches:
        fetch.start()
    queries, new_keys, new_values, keys, values = held
    fetches[0].wait()
    for device in range(DEVICES):
        at = ((device >> 5) * 4 + (device & 3)) * 256
        send[device] = queries[:, at : at + 256]
    width = KV_HEADS * HEAD
    fetches[1].wait()
    fetches[2].wait()
    live = jnp.full((8, width), live_ref[0].astype(f32))
    gap = jnp.zeros((4, width), f32)
    tail[0:16, :] = jnp.concatenate([new_keys[...].astype(f32), gap, live], axis=0).astype(bf16)
    tail[16:32, :] = jnp.concatenate([new_values[...].astype(f32), gap, gap, gap], axis=0).astype(bf16)
    head = head_ref[0]
    columns = [pl.ds(pl.multiple_of((head ^ d) * HEAD, HEAD), HEAD) for d in range(8)]
    for d in range(8):
        pieces[d][2 * KEYS : PIECE, :] = tail[:, columns[d]]
    fetches[3].wait()
    for d in range(8):
        pieces[d][0:KEYS, :] = keys[:, columns[d]]
    fetches[4].wait()
    for d in range(8):
        pieces[d][KEYS : 2 * KEYS, :] = values[:, columns[d]]


def pack(head, live, queries, new_keys, new_values, keys, values):
    whole = pl.BlockSpec(memory_space=pltpu.VMEM)
    return pl.pallas_call(
        pack_kernel,
        out_shape=[jax.ShapeDtypeStruct((DEVICES, SLOTS, 256), jnp.bfloat16)]
        + [jax.ShapeDtypeStruct((PIECE, HEAD), jnp.bfloat16)] * 8,
        in_specs=[pl.BlockSpec(memory_space=pltpu.SMEM)] * 2
        + [pl.BlockSpec(memory_space=pltpu.HBM)] * 5,
        out_specs=[whole] * 9,
        scratch_shapes=[
            pltpu.VMEM((32, KV_HEADS * HEAD), jnp.bfloat16),
            pltpu.VMEM((SLOTS, 4096), jnp.bfloat16),
            pltpu.VMEM((SLOTS, KV_HEADS * HEAD), jnp.bfloat16),
            pltpu.VMEM((SLOTS, KV_HEADS * HEAD), jnp.bfloat16),
            pltpu.VMEM((KEYS, KV_HEADS * HEAD), jnp.bfloat16),
            pltpu.VMEM((KEYS, KV_HEADS * HEAD), jnp.bfloat16),
            pltpu.SemaphoreType.DMA((5,)),
        ],
        compiler_params=pltpu.CompilerParams(vmem_limit_bytes=PACK_LIMIT << 20),
        cost_estimate=pl.CostEstimate(flops=0, bytes_accessed=2 << 20, transcendentals=0),
        name="pack",
    )(head, live, queries, new_keys, new_values, keys, values)


def prepare_kernel(here_ref, col_ref, row_ref, *rest):
    pieces, (pick, near, far, token_ref, tails) = rest[:EARLY], rest[EARLY:]
    f32, bf16, i32 = jnp.float32, jnp.bfloat16, jnp.int32
    here = here_ref[0]
    iota = lambda shape, dim: lax.broadcasted_iota(i32, shape, dim)
    own_col, own_row = col_ref[...], row_ref[...]

    same = own_col == own_row
    down, across = iota((TOKENS, TOKENS), 0), iota((TOKENS, TOKENS), 1)
    rank_col = jnp.sum(jnp.where(same & (across < down), 1.0, 0.0), axis=1, keepdims=True)
    rank_row = jnp.sum(jnp.where(same & (down < across), 1.0, 0.0), axis=0, keepdims=True)
    place_col = own_col * SLOTS + rank_col.astype(i32)
    place_row = own_row * SLOTS + rank_row.astype(i32)

    pick[...] = jnp.where(place_col == iota((TOKENS, DEVICES * SLOTS), 1), 1.0, 0.0).astype(bf16)
    line = (down >> 1) * SLOTS + (down & 1)
    near[...] = jnp.where(line == place_row, 1.0, 0.0).astype(bf16)
    far[...] = jnp.where(line + 2 == place_row, 1.0, 0.0).astype(bf16)

    column = iota((1, KEYS), 1)
    part, row = column >> 4, column & 15
    chip = jnp.zeros_like(part)
    for number, d in enumerate(ORDER):
        chip = jnp.where((part & 7) == number, CHIP_MASKS[d], chip)
    device = here ^ (chip + (part >> 3))
    slot = jnp.where(row < SLOTS, device * SLOTS + row, -1)
    token = jnp.where(place_col == slot, down.astype(f32) + 1.0, 0.0)
    token_ref[...] = jnp.sum(token, axis=0, keepdims=True) - 1.0

    for p in range(EARLY):
        tails[32 * p : 32 * p + 32, :] = pieces[p][2 * KEYS : PIECE, :]


def prepare(here, own_col, own_row, pieces):
    whole = pl.BlockSpec(memory_space=pltpu.VMEM)
    shape = jax.ShapeDtypeStruct
    return pl.pallas_call(
        prepare_kernel,
        out_shape=[
            shape((TOKENS, DEVICES * SLOTS), jnp.bfloat16),
            shape((TOKENS, TOKENS), jnp.bfloat16),
            shape((TOKENS, TOKENS), jnp.bfloat16),
            shape((1, KEYS), jnp.float32),
            shape((32 * EARLY, HEAD), jnp.bfloat16),
        ],
        in_specs=[pl.BlockSpec(memory_space=pltpu.SMEM)] + [whole] * (2 + EARLY),
        out_specs=[whole] * 5,
        compiler_params=pltpu.CompilerParams(vmem_limit_bytes=8 << 20),
        cost_estimate=pl.CostEstimate(flops=PREPARE_FLOPS, bytes_accessed=1 << 19, transcendentals=0),
        name="prepare",
    )(here, own_col, own_row, *pieces)


def attend_kernel(q_ref, pick, near, far, token_ref, tails, *rest):
    pieces, out_ref = rest[:16], rest[16]
    scores, new_keys, new_values = rest[17:]
    f32, bf16 = jnp.float32, jnp.bfloat16
    iota = lambda shape, dim: lax.broadcasted_iota(jnp.int32, shape, dim)

    by_token = jnp.dot(pick[...], q_ref[...], preferred_element_type=f32).astype(bf16)

    lane_bias = []
    for p in range(16):
        tail = pieces[p][2 * KEYS : PIECE, :] if p >= EARLY else tails[32 * p : 32 * p + 32, :]
        new_keys[16 * p : 16 * p + 16, :] = tail[0:16]
        new_values[16 * p : 16 * p + 16, :] = tail[16:32]
        live = tail[0:16].astype(f32)[8:9, 0:1]
        lane_bias.append(jnp.where(iota((1, KEYS), 1).astype(f32) < live, 0.0, HIDDEN))

    token = token_ref[...]
    contract = (((1,), (1,)), ((), ()))
    peaks = []
    for b in range(2):
        head, start = b, 0
        plain = by_token[start : start + BLOCK, head * HEAD : (head + 1) * HEAD]
        peak = jnp.full((BLOCK, HEAD), HIDDEN, f32)
        for p in range(16):
            score = lax.dot_general(
                plain, pieces[p][0:KEYS, :], contract, preferred_element_type=f32
            )
            score = score + lane_bias[p]
            scores[b, p] = score
            peak = jnp.maximum(peak, jnp.maximum(score[:, :HEAD], score[:, HEAD:]))
        reader = (iota((BLOCK, 1), 0) + start).astype(f32)
        seen = (token >= 0.0) & (token <= reader)
        score = lax.dot_general(plain, new_keys[...], contract, preferred_element_type=f32)
        score = jnp.where(seen, score, HIDDEN)
        scores[b, 16] = score
        peak = jnp.maximum(peak, jnp.maximum(score[:, :HEAD], score[:, HEAD:]))
        peaks.append(jnp.max(peak, axis=1, keepdims=True))

    totals, sums = [], []
    for b in range(2):
        total = jnp.zeros((BLOCK, HEAD), f32)
        mixed = jnp.zeros((BLOCK, HEAD), f32)
        for p in range(CHUNKS):
            weight = jnp.exp2((scores[b, p] - peaks[b]) * SCALE)
            total = total + (weight[:, :HEAD] + weight[:, HEAD:])
            value = new_values[...] if p == 16 else pieces[p][KEYS : 2 * KEYS, :]
            mixed = mixed + jnp.dot(weight.astype(bf16), value, preferred_element_type=f32)
        totals.append(jnp.sum(total, axis=1, keepdims=True))
        sums.append(mixed)
    peak, total = jnp.concatenate(peaks, axis=0), jnp.concatenate(totals, axis=0)
    mean = jnp.concatenate(sums, axis=0) / total

    reach = jnp.max(jnp.abs(mean), axis=1, keepdims=True)
    step = jnp.round(jnp.log2(jnp.maximum(reach, 1e-30)))
    mean = mean * jnp.exp2(-step)
    rough = mean.astype(bf16)
    fine = (mean - rough.astype(f32)).astype(bf16)
    level = peak * SCALE + jnp.log2(total)
    high = level.astype(bf16).astype(f32)
    middle = (level - high).astype(bf16).astype(f32)
    low = level - high - middle
    place = iota((TOKENS, HEAD), 1) & 63
    parts = jnp.zeros((TOKENS, HEAD), f32)
    for number, value in enumerate((high, middle, low, step)):
        parts = jnp.where(place == 2 * number, value[:TOKENS], parts)
        parts = jnp.where(place == 2 * number + 1, value[TOKENS:], parts)
    whole = jnp.concatenate(
        [rough[:TOKENS], rough[TOKENS:], fine[:TOKENS], fine[TOKENS:], parts.astype(bf16)], axis=1
    )

    first = jnp.dot(near[...], whole, preferred_element_type=f32)
    second = jnp.dot(far[...], whole, preferred_element_type=f32)
    out_ref[:, 0:256] = first[:, 0:256] + first[:, 256:512]
    out_ref[:, 256:512] = second[:, 0:256] + second[:, 256:512]
    out_ref[:, 512:640] = jnp.where(iota((TOKENS, HEAD), 1) < 64, first[:, 512:], second[:, 512:])


def attend(queries, prepared, pieces):
    whole = pl.BlockSpec(memory_space=pltpu.VMEM)
    return pl.pallas_call(
        attend_kernel,
        out_shape=jax.ShapeDtypeStruct((TOKENS, 640), jnp.float32),
        in_specs=[whole] * 22,
        out_specs=whole,
        scratch_shapes=[
            pltpu.VMEM((2, CHUNKS, BLOCK, KEYS), jnp.float32),
            pltpu.VMEM((KEYS, HEAD), jnp.bfloat16),
            pltpu.VMEM((KEYS, HEAD), jnp.bfloat16),
        ],
        compiler_params=pltpu.CompilerParams(vmem_limit_bytes=20 << 20),
        cost_estimate=pl.CostEstimate(
            flops=4 * 512 * 4352 * 128, bytes_accessed=3 << 20, transcendentals=512 * 4352
        ),
        name="attend",
    )(queries, *prepared, *pieces)


def combine_kernel(parts_ref, out_ref, whole):
    split = lambda array: array.reshape(4, 8, 4, 2, array.shape[-1])
    levels = parts_ref[:, :, 512:640]
    ahead = lambda count: pltpu.roll(levels, HEAD - count, 2)
    step = jnp.exp2(ahead(6))
    level = split(levels + ahead(2) + ahead(4))
    factor = jnp.exp2(level - jnp.max(level, axis=1, keepdims=True))
    factor = factor / jnp.sum(factor, axis=1, keepdims=True) * split(step)
    for v in range(4):
        at = 64 * (v // 2) + v % 2
        mean = split(parts_ref[:, :, v * HEAD : (v + 1) * HEAD])
        mean = jnp.sum(mean * factor[..., at : at + 1], axis=1).reshape(16, 2, HEAD)
        for pair in range(16):
            column = pair * 256 + v % 2 * HEAD
            whole[v // 2 * 2 : v // 2 * 2 + 2, column : column + HEAD] = mean[pair]
    out_ref[...] = whole[...].astype(jnp.bfloat16)


def combine(parts):
    whole = pl.BlockSpec(memory_space=pltpu.VMEM)
    return pl.pallas_call(
        combine_kernel,
        out_shape=jax.ShapeDtypeStruct((SLOTS, 4096), jnp.bfloat16),
        in_specs=[whole],
        out_specs=whole,
        scratch_shapes=[pltpu.VMEM((SLOTS, 4096), jnp.float32)],
        compiler_params=pltpu.CompilerParams(vmem_limit_bytes=16 << 20),
        name="combine",
    )(parts)


def per_device(queries, owners, new_keys, new_values, cache_keys, cache_values, lengths):
    bf16 = jnp.bfloat16
    here = lax.axis_index("ctx").astype(jnp.int32)
    head = (here >> 5) * 2 + (here >> 1 & 1)

    send, *mine = pack(head[None], lengths, queries, new_keys, new_values, cache_keys, cache_values)
    held = [mine[0]]
    for number, d in enumerate(ORDER[1:], 1):
        piece = mine[d]
        if AFTER[number]:
            piece, _ = lax.optimization_barrier((piece, held[AFTER[number]]))
        held.append(swap(piece, CHIP_MASKS[d]))
    other = [swap(piece, 1) for piece in held]
    everyone = lax.all_to_all(send, "ctx", 0, 0).reshape(DEVICES * SLOTS, 256)
    prepared = prepare(here[None], owners, owners.reshape(1, TOKENS), held[:EARLY])
    partial = attend(everyone, prepared, held + other)
    partial = partial.astype(jnp.float16).reshape(DEVICES, 2, 640)
    return combine(lax.all_to_all(partial, "ctx", 0, 0).astype(jnp.float32))


def solution(mesh):
    return jax.shard_map(
        per_device,
        mesh=mesh,
        in_specs=(
            P(("batch", "ctx"), None),
            P("batch", None),
            P(("batch", "ctx"), None),
            P(("batch", "ctx"), None),
            P(("batch", "ctx"), None),
            P(("batch", "ctx"), None),
            P(("batch", "ctx")),
        ),
        out_specs=P(("batch", "ctx"), None),
        check_vma=False,
    )
```

```python
import math

import jax
import jax.numpy as jnp
from jax import lax
from jax.experimental import pallas as pl
from jax.experimental.pallas import tpu as pltpu
from jax.sharding import PartitionSpec as P

HEAD = 128
KV_HEADS = 8
SLOTS = 4
TOKENS = 256
KEYS = 256
DEVICES = 128
CHIP_MASKS = tuple((d >> 1) * 32 + (d & 1) * 2 for d in range(8))
ORDER = (0, 7, 3, 5, 4, 1, 6, 2)
EARLY = 4
AFTER = (0, 0, 0, 0, 0, 2, 3, 4)
PREPARE_FLOPS = 2850000000
PACK_LIMIT = 56
PIECE = 2 * KEYS + 32
CHUNKS = 17
BLOCK = 256
SCALE = math.log2(math.e) / math.sqrt(HEAD)
HIDDEN = -1e30


def swap(array, mask):
    return lax.ppermute(array, "ctx", [(i, i ^ mask) for i in range(DEVICES)])


def pack_kernel(head_ref, live_ref, *rest):
    given, send, pieces, tail, held, sems = rest[:5], rest[5], rest[6:14], rest[14], rest[15:20], rest[20]
    f32, bf16 = jnp.float32, jnp.bfloat16
    fetches = [pltpu.make_async_copy(given[i], held[i], sems.at[i]) for i in range(5)]
    for fetch in fetches:
        fetch.start()
    queries, new_keys, new_values, keys, values = held
    fetches[0].wait()
    for device in range(DEVICES):
        at = ((device >> 5) * 4 + (device & 3)) * 256
        send[device] = queries[:, at : at + 256]
    width = KV_HEADS * HEAD
    fetches[1].wait()
    fetches[2].wait()
    live = jnp.full((8, width), live_ref[0].astype(f32))
    gap = jnp.zeros((4, width), f32)
    tail[0:16, :] = jnp.concatenate([new_keys[...].astype(f32), gap, live], axis=0).astype(bf16)
    tail[16:32, :] = jnp.concatenate([new_values[...].astype(f32), gap, gap, gap], axis=0).astype(bf16)
    head = head_ref[0]
    columns = [pl.ds(pl.multiple_of((head ^ d) * HEAD, HEAD), HEAD) for d in range(8)]
    for d in range(8):
        pieces[d][2 * KEYS : PIECE, :] = tail[:, columns[d]]
    fetches[3].wait()
    for d in range(8):
        pieces[d][0:KEYS, :] = keys[:, columns[d]]
    fetches[4].wait()
    for d in range(8):
        pieces[d][KEYS : 2 * KEYS, :] = values[:, columns[d]]


def pack(head, live, queries, new_keys, new_values, keys, values):
    whole = pl.BlockSpec(memory_space=pltpu.VMEM)
    return pl.pallas_call(
        pack_kernel,
        out_shape=[jax.ShapeDtypeStruct((DEVICES, SLOTS, 256), jnp.bfloat16)]
        + [jax.ShapeDtypeStruct((PIECE, HEAD), jnp.bfloat16)] * 8,
        in_specs=[pl.BlockSpec(memory_space=pltpu.SMEM)] * 2
        + [pl.BlockSpec(memory_space=pltpu.HBM)] * 5,
        out_specs=[whole] * 9,
        scratch_shapes=[
            pltpu.VMEM((32, KV_HEADS * HEAD), jnp.bfloat16),
            pltpu.VMEM((SLOTS, 4096), jnp.bfloat16),
            pltpu.VMEM((SLOTS, KV_HEADS * HEAD), jnp.bfloat16),
            pltpu.VMEM((SLOTS, KV_HEADS * HEAD), jnp.bfloat16),
            pltpu.VMEM((KEYS, KV_HEADS * HEAD), jnp.bfloat16),
            pltpu.VMEM((KEYS, KV_HEADS * HEAD), jnp.bfloat16),
            pltpu.SemaphoreType.DMA((5,)),
        ],
        compiler_params=pltpu.CompilerParams(vmem_limit_bytes=PACK_LIMIT << 20),
        cost_estimate=pl.CostEstimate(flops=0, bytes_accessed=2 << 20, transcendentals=0),
        name="pack",
    )(head, live, queries, new_keys, new_values, keys, values)


def prepare_kernel(here_ref, col_ref, row_ref, *rest):
    pieces, (pick, near, far, token_ref, tails) = rest[:EARLY], rest[EARLY:]
    f32, bf16, i32 = jnp.float32, jnp.bfloat16, jnp.int32
    here = here_ref[0]
    iota = lambda shape, dim: lax.broadcasted_iota(i32, shape, dim)
    own_col, own_row = col_ref[...], row_ref[...]

    same = own_col == own_row
    down, across = iota((TOKENS, TOKENS), 0), iota((TOKENS, TOKENS), 1)
    rank_col = jnp.sum(jnp.where(same & (across < down), 1.0, 0.0), axis=1, keepdims=True)
    rank_row = jnp.sum(jnp.where(same & (down < across), 1.0, 0.0), axis=0, keepdims=True)
    place_col = own_col * SLOTS + rank_col.astype(i32)
    place_row = own_row * SLOTS + rank_row.astype(i32)

    pick[...] = jnp.where(place_col == iota((TOKENS, DEVICES * SLOTS), 1), 1.0, 0.0).astype(bf16)
    line = (down >> 1) * SLOTS + (down & 1)
    near[...] = jnp.where(line == place_row, 1.0, 0.0).astype(bf16)
    far[...] = jnp.where(line + 2 == place_row, 1.0, 0.0).astype(bf16)

    column = iota((1, KEYS), 1)
    part, row = column >> 4, column & 15
    chip = jnp.zeros_like(part)
    for number, d in enumerate(ORDER):
        chip = jnp.where((part & 7) == number, CHIP_MASKS[d], chip)
    device = here ^ (chip + (part >> 3))
    slot = jnp.where(row < SLOTS, device * SLOTS + row, -1)
    token = jnp.where(place_col == slot, down.astype(f32) + 1.0, 0.0)
    token_ref[...] = jnp.sum(token, axis=0, keepdims=True) - 1.0

    for p in range(EARLY):
        tails[32 * p : 32 * p + 32, :] = pieces[p][2 * KEYS : PIECE, :]


def prepare(here, own_col, own_row, pieces):
    whole = pl.BlockSpec(memory_space=pltpu.VMEM)
    shape = jax.ShapeDtypeStruct
    return pl.pallas_call(
        prepare_kernel,
        out_shape=[
            shape((TOKENS, DEVICES * SLOTS), jnp.bfloat16),
            shape((TOKENS, TOKENS), jnp.bfloat16),
            shape((TOKENS, TOKENS), jnp.bfloat16),
            shape((1, KEYS), jnp.float32),
            shape((32 * EARLY, HEAD), jnp.bfloat16),
        ],
        in_specs=[pl.BlockSpec(memory_space=pltpu.SMEM)] + [whole] * (2 + EARLY),
        out_specs=[whole] * 5,
        compiler_params=pltpu.CompilerParams(vmem_limit_bytes=8 << 20),
        cost_estimate=pl.CostEstimate(flops=PREPARE_FLOPS, bytes_accessed=1 << 19, transcendentals=0),
        name="prepare",
    )(here, own_col, own_row, *pieces)


def attend_kernel(q_ref, pick, near, far, token_ref, tails, *rest):
    pieces, out_ref = rest[:16], rest[16]
    scores, new_keys, new_values = rest[17:]
    f32, bf16 = jnp.float32, jnp.bfloat16
    iota = lambda shape, dim: lax.broadcasted_iota(jnp.int32, shape, dim)

    by_token = jnp.dot(pick[...], q_ref[...], preferred_element_type=f32).astype(bf16)

    lane_bias = []
    for p in range(16):
        tail = pieces[p][2 * KEYS : PIECE, :] if p >= EARLY else tails[32 * p : 32 * p + 32, :]
        new_keys[16 * p : 16 * p + 16, :] = tail[0:16]
        new_values[16 * p : 16 * p + 16, :] = tail[16:32]
        live = tail[0:16].astype(f32)[8:9, 0:1]
        lane_bias.append(jnp.where(iota((1, KEYS), 1).astype(f32) < live, 0.0, HIDDEN))

    token = token_ref[...]
    contract = (((1,), (1,)), ((), ()))
    peaks = []
    for b in range(2):
        head, start = b, 0
        plain = by_token[start : start + BLOCK, head * HEAD : (head + 1) * HEAD]
        peak = jnp.full((BLOCK, HEAD), HIDDEN, f32)
        for p in range(16):
            score = lax.dot_general(
                plain, pieces[p][0:KEYS, :], contract, preferred_element_type=f32
            )
            score = score + lane_bias[p]
            scores[b, p] = score
            peak = jnp.maximum(peak, jnp.maximum(score[:, :HEAD], score[:, HEAD:]))
        reader = (iota((BLOCK, 1), 0) + start).astype(f32)
        seen = (token >= 0.0) & (token <= reader)
        score = lax.dot_general(plain, new_keys[...], contract, preferred_element_type=f32)
        score = jnp.where(seen, score, HIDDEN)
        scores[b, 16] = score
        peak = jnp.maximum(peak, jnp.maximum(score[:, :HEAD], score[:, HEAD:]))
        peaks.append(jnp.max(peak, axis=1, keepdims=True))

    totals, sums = [], []
    for b in range(2):
        total = jnp.zeros((BLOCK, HEAD), f32)
        mixed = jnp.zeros((BLOCK, HEAD), f32)
        for p in range(CHUNKS):
            weight = jnp.exp2((scores[b, p] - peaks[b]) * SCALE)
            total = total + (weight[:, :HEAD] + weight[:, HEAD:])
            value = new_values[...] if p == 16 else pieces[p][KEYS : 2 * KEYS, :]
            mixed = mixed + jnp.dot(weight.astype(bf16), value, preferred_element_type=f32)
        totals.append(jnp.sum(total, axis=1, keepdims=True))
        sums.append(mixed)
    peak, total = jnp.concatenate(peaks, axis=0), jnp.concatenate(totals, axis=0)
    mean = jnp.concatenate(sums, axis=0) / total

    reach = jnp.max(jnp.abs(mean), axis=1, keepdims=True)
    step = jnp.round(jnp.log2(jnp.maximum(reach, 1e-30)))
    mean = mean * jnp.exp2(-step)
    rough = mean.astype(bf16)
    fine = (mean - rough.astype(f32)).astype(bf16)
    level = peak * SCALE + jnp.log2(total)
    high = level.astype(bf16).astype(f32)
    middle = (level - high).astype(bf16).astype(f32)
    low = level - high - middle
    place = iota((TOKENS, HEAD), 1) & 63
    parts = jnp.zeros((TOKENS, HEAD), f32)
    for number, value in enumerate((high, middle, low, step)):
        parts = jnp.where(place == 2 * number, value[:TOKENS], parts)
        parts = jnp.where(place == 2 * number + 1, value[TOKENS:], parts)
    whole = jnp.concatenate(
        [rough[:TOKENS], rough[TOKENS:], fine[:TOKENS], fine[TOKENS:], parts.astype(bf16)], axis=1
    )

    first = jnp.dot(near[...], whole, preferred_element_type=f32)
    second = jnp.dot(far[...], whole, preferred_element_type=f32)
    out_ref[:, 0:256] = first[:, 0:256] + first[:, 256:512]
    out_ref[:, 256:512] = second[:, 0:256] + second[:, 256:512]
    out_ref[:, 512:640] = jnp.where(iota((TOKENS, HEAD), 1) < 64, first[:, 512:], second[:, 512:])


def attend(queries, prepared, pieces):
    whole = pl.BlockSpec(memory_space=pltpu.VMEM)
    return pl.pallas_call(
        attend_kernel,
        out_shape=jax.ShapeDtypeStruct((TOKENS, 640), jnp.float32),
        in_specs=[whole] * 22,
        out_specs=whole,
        scratch_shapes=[
            pltpu.VMEM((2, CHUNKS, BLOCK, KEYS), jnp.float32),
            pltpu.VMEM((KEYS, HEAD), jnp.bfloat16),
            pltpu.VMEM((KEYS, HEAD), jnp.bfloat16),
        ],
        compiler_params=pltpu.CompilerParams(vmem_limit_bytes=20 << 20),
        cost_estimate=pl.CostEstimate(
            flops=4 * 512 * 4352 * 128, bytes_accessed=3 << 20, transcendentals=512 * 4352
        ),
        name="attend",
    )(queries, *prepared, *pieces)


def combine_kernel(parts_ref, out_ref, whole):
    split = lambda array: array.reshape(4, 8, 4, 2, array.shape[-1])
    levels = parts_ref[:, :, 512:640]
    ahead = lambda count: pltpu.roll(levels, HEAD - count, 2)
    step = jnp.exp2(ahead(6))
    level = split(levels + ahead(2) + ahead(4))
    factor = jnp.exp2(level - jnp.max(level, axis=1, keepdims=True))
    total = jnp.sum(factor, axis=1).reshape(16, 2, HEAD)
    factor = factor * split(step)
    for v in range(4):
        at = 64 * (v // 2) + v % 2
        mean = split(parts_ref[:, :, v * HEAD : (v + 1) * HEAD])
        mean = jnp.sum(mean * factor[..., at : at + 1], axis=1).reshape(16, 2, HEAD)
        mean = mean / total[..., at : at + 1]
        for pair in range(16):
            column = pair * 256 + v % 2 * HEAD
            whole[v // 2 * 2 : v // 2 * 2 + 2, column : column + HEAD] = mean[pair]
    out_ref[...] = whole[...].astype(jnp.bfloat16)


def combine(parts):
    whole = pl.BlockSpec(memory_space=pltpu.VMEM)
    return pl.pallas_call(
        combine_kernel,
        out_shape=jax.ShapeDtypeStruct((SLOTS, 4096), jnp.bfloat16),
        in_specs=[whole],
        out_specs=whole,
        scratch_shapes=[pltpu.VMEM((SLOTS, 4096), jnp.float32)],
        compiler_params=pltpu.CompilerParams(vmem_limit_bytes=16 << 20),
        name="combine",
    )(parts)


def per_device(queries, owners, new_keys, new_values, cache_keys, cache_values, lengths):
    bf16 = jnp.bfloat16
    here = lax.axis_index("ctx").astype(jnp.int32)
    head = (here >> 5) * 2 + (here >> 1 & 1)

    send, *mine = pack(head[None], lengths, queries, new_keys, new_values, cache_keys, cache_values)
    held = [mine[0]]
    for number, d in enumerate(ORDER[1:], 1):
        piece = mine[d]
        if AFTER[number]:
            piece, _ = lax.optimization_barrier((piece, held[AFTER[number]]))
        held.append(swap(piece, CHIP_MASKS[d]))
    other = [swap(piece, 1) for piece in held]
    everyone = lax.all_to_all(send, "ctx", 0, 0).reshape(DEVICES * SLOTS, 256)
    prepared = prepare(here[None], owners, owners.reshape(1, TOKENS), held[:EARLY])
    partial = attend(everyone, prepared, held + other)
    partial = partial.astype(jnp.float16).reshape(DEVICES, 2, 640)
    return combine(lax.all_to_all(partial, "ctx", 0, 0).astype(jnp.float32))


def solution(mesh):
    return jax.shard_map(
        per_device,
        mesh=mesh,
        in_specs=(
            P(("batch", "ctx"), None),
            P("batch", None),
            P(("batch", "ctx"), None),
            P(("batch", "ctx"), None),
            P(("batch", "ctx"), None),
            P(("batch", "ctx"), None),
            P(("batch", "ctx")),
        ),
        out_specs=P(("batch", "ctx"), None),
        check_vma=False,
    )
```
